32 devices in a mesh: groups: 2 (over y), band: 4 (over x, core), sect: 4 (over z).
Axes of the slice: x: 2, y: 2, z: 4, core: 2. Of those that a mesh axis runs over, the one named last changes fastest.
Arguments:
- state_field: bfloat16 [198, 128, 512], P('groups', 'band', 'sect'), parts along dimension 0, may hold values from -6 to 6
- conv_in_weight: bfloat16 [9, 128, 99], replicated, may hold values from -0.1875 to 0.1875
- conv_in_bias: float32 [128], replicated, may hold values from -3 to 3
- conv_out_weight: bfloat16 [9, 99, 128], replicated, may hold values from -0.1875 to 0.1875
- conv_out_bias: float32 [99], replicated, may hold values from -3 to 3
- patch_anchor: int32 [32, 2], P('groups'), parts along dimension 0, may hold values from 0 to 480, as said below
- patch_noise: bfloat16 [32, 2, 99, 1024], P(('groups', 'band', 'sect')), parts along dimension 0, may hold values from -6 to 6
- denoise_in_weight: bfloat16 [9, 128, 99], replicated, may hold values from -0.1875 to 0.1875
- step_bias: float32 [2, 128], replicated, may hold values from -3 to 3
- denoise_out_weight: bfloat16 [9, 99, 128], replicated, may hold values from -0.1875 to 0.1875
- denoise_bias: float32 [99], replicated, may hold values from -3 to 3
Outputs:
- next_field: bfloat16 [198, 128, 512], P('groups', 'band', 'sect'), parts along dimension 0
The draws below stay inside these ranges and needn't reach their ends.
There are 2 independent parts, one for each index of `groups`. The reference program is written for one: setup_inputs(seed, part) draws one part's arguments, and reference() takes and returns one part's arrays. A program takes and returns all parts, laid end to end along the dimension named above; an argument that names none is the same for every part. Nothing has to cross between parts.
Inputs may be any that keep to these rules, and one draw needn't show every extreme that they name: `patch_anchor`: patches p * 1 to p + 1 - 1 are denoised by the device at position p of band+sect, band first. Each patch's anchor column lies in the columns of its reader's sector, its anchor row at most 96 and its anchor column at most 480. Among the patches of one sector, at most 2 have anchor rows in one band's rows, and in every sector some band holds exactly 2.
All inputs are finite; a program needn't handle non-finite values.
Results may differ from the reference program's by a relative error of at most 0.0049.
Values may be sent and summed in bfloat16 or wider, within the bound.
A program may use at most 64 MiB of HBM per device.

```python
import jax
import jax.numpy as jnp
from jax import lax

CH = 99
HID = 128
RB = 32
CB = 128
P_SIZE = 32
PPD = 1
STEPS = 2
NLAT = 128
NLON = 512
NP = 16
N_BAND = 4
N_SECT = 4


def draw_patch_anchor(key, part):
    keys = jax.random.split(jax.random.fold_in(key, 17), 5)
    band_total = N_BAND
    sect_total = N_SECT
    owner_perm = jax.vmap(lambda sub: jax.random.permutation(sub, band_total))(jax.random.split(keys[0], sect_total))
    unit_perm = jax.vmap(lambda sub: jax.random.permutation(sub, band_total))(jax.random.split(keys[1], sect_total))
    doubled = jax.random.randint(keys[2], (sect_total,), 1, band_total // 2 + 1)
    position = jnp.arange(band_total, dtype=jnp.int32)
    mapped = jnp.where(position[None, :] < 2 * doubled[:, None], position[None, :] // 2, position[None, :])
    chosen = jnp.take_along_axis(mapped, unit_perm, axis=1)
    owner = jnp.take_along_axis(owner_perm, chosen, axis=1)
    owner_grid = jnp.broadcast_to(owner.T[:, :, None], (band_total, sect_total, PPD))
    sector = jnp.broadcast_to(jnp.arange(sect_total, dtype=jnp.int32)[None, :, None], (band_total, sect_total, PPD))
    row_offset = jax.random.randint(keys[3], (band_total, sect_total, PPD), 0, RB)
    col_offset = jax.random.randint(keys[4], (band_total, sect_total, PPD), 0, CB)
    anchor_rows = jnp.minimum(owner_grid * RB + row_offset, NLAT - P_SIZE)
    anchor_cols = jnp.minimum(sector * CB + col_offset, NLON - P_SIZE)
    return jnp.stack([anchor_rows, anchor_cols], axis=-1).reshape(NP, 2).astype(jnp.int32)


def block_scale(stream_key, extent, shards, low, largest):
    def one(axis_at, parts):
        draws = jax.random.uniform(jax.random.fold_in(jax.random.fold_in(stream_key, 6), axis_at), (parts,), jnp.float32, low / len(shards), largest / len(shards))
        return jnp.repeat(jnp.exp(draws), extent[axis_at] // parts).reshape((-1,) + (1,) * (len(extent) - axis_at - 1))

    level = one(*shards[0])
    for cut in shards[1:]:
        level = level * one(*cut)
    return level


def gaussian(stream_key, dims, spread, limit, cuts=(), kind=jnp.bfloat16):
    factor_of = block_scale(stream_key, dims, cuts, -0.22, 0.18) if cuts else 1.0
    values = jax.random.normal(stream_key, dims, jnp.float32) * spread * factor_of
    return jnp.minimum(jnp.maximum(values, -limit), limit).astype(kind)


def setup_inputs(seed: int = 0, part: int = 0) -> dict:
    streams_of = jax.random.split(jax.random.key(seed), 12)
    own_keys = jax.random.split(jax.random.fold_in(streams_of[11], part), 12)
    return {
        "state_field": gaussian(own_keys[0], (CH, NLAT, NLON), 1.0, 6.0, ((1, 4), (2, 4))),
        "conv_in_weight": gaussian(streams_of[1], (9, HID, CH), (9 * CH) ** -0.5, 0.1875),
        "conv_in_bias": gaussian(streams_of[2], (HID,), 0.5, 3.0, (), jnp.float32),
        "conv_out_weight": gaussian(streams_of[3], (9, CH, HID), (9 * HID) ** -0.5, 0.1875),
        "conv_out_bias": gaussian(streams_of[4], (CH,), 0.5, 3.0, (), jnp.float32),
        "patch_anchor": draw_patch_anchor(jax.random.fold_in(jax.random.fold_in(streams_of[11], part), 71), part),
        "patch_noise": gaussian(own_keys[6], (NP, STEPS, CH, P_SIZE * P_SIZE), 1.0, 6.0, ((0, 16),)),
        "denoise_in_weight": gaussian(streams_of[7], (9, HID, CH), (9 * CH) ** -0.5, 0.1875),
        "step_bias": gaussian(streams_of[8], (STEPS, HID), 0.5, 3.0, (), jnp.float32),
        "denoise_out_weight": gaussian(streams_of[9], (9, CH, HID), (9 * HID) ** -0.5, 0.1875),
        "denoise_bias": gaussian(streams_of[10], (CH,), 0.5, 3.0, (), jnp.float32),
    }


def conv_grid(values, weight):
    height = values.shape[1]
    width = values.shape[2]
    padded = jnp.pad(values, ((0, 0), (1, 1), (1, 1)))
    summed = jnp.zeros((weight.shape[1], height, width), jnp.float32)
    tap_index = 0
    for shift_row in (-1, 0, 1):
        for shift_col in (-1, 0, 1):
            window = padded[:, 1 + shift_row:1 + shift_row + height, 1 + shift_col:1 + shift_col + width]
            summed = summed + jnp.einsum("oi,ihw->ohw", weight[tap_index].astype(jnp.float32), window.astype(jnp.float32))
            tap_index = tap_index + 1
    return summed


def reference(state_field, conv_in_weight, conv_in_bias, conv_out_weight, conv_out_bias, patch_anchor, patch_noise, denoise_in_weight, step_bias, denoise_out_weight, denoise_bias):
    hidden = jax.nn.silu(conv_grid(state_field, conv_in_weight) + conv_in_bias[:, None, None]).astype(jnp.bfloat16)
    mean_field = (state_field.astype(jnp.float32) + conv_grid(hidden, conv_out_weight) + conv_out_bias[:, None, None]).astype(jnp.bfloat16)
    noises = patch_noise.reshape(NP, STEPS, CH, P_SIZE, P_SIZE)

    def one_patch(inputs):
        anchor, noise_set = inputs
        zero = jnp.zeros((), jnp.int32)
        patch_mean = lax.dynamic_slice(mean_field, (zero, anchor[0].astype(jnp.int32), anchor[1].astype(jnp.int32)), (CH, P_SIZE, P_SIZE))
        state = patch_mean.astype(jnp.float32) + noise_set[0].astype(jnp.float32)
        for step in range(STEPS):
            inner = state.astype(jnp.bfloat16)
            denoise_hidden = jax.nn.silu(conv_grid(inner, denoise_in_weight) + step_bias[step][:, None, None]).astype(jnp.bfloat16)
            state = state - 0.5 * (conv_grid(denoise_hidden, denoise_out_weight) + denoise_bias[:, None, None])
            if step + 1 < STEPS:
                state = state + 0.5 * noise_set[step + 1].astype(jnp.float32)
        return (state - patch_mean.astype(jnp.float32)).astype(jnp.bfloat16)

    corrections = lax.map(one_patch, (patch_anchor, noises))

    def accumulate(index, canvas):
        anchor = patch_anchor[index]
        zero = jnp.zeros((), jnp.int32)
        start = (zero, anchor[0].astype(jnp.int32), anchor[1].astype(jnp.int32))
        current = lax.dynamic_slice(canvas, start, (CH, P_SIZE, P_SIZE))
        return lax.dynamic_update_slice(canvas, current + corrections[index].astype(jnp.float32), start)

    summed = lax.fori_loop(0, NP, accumulate, jnp.zeros((CH, NLAT, NLON), jnp.float32))
    grid_rows = jnp.arange(NLAT, dtype=jnp.int32)
    grid_cols = jnp.arange(NLON, dtype=jnp.int32)
    start_rows = patch_anchor[:, 0:1]
    start_cols = patch_anchor[:, 1:2]
    cover_rows = ((grid_rows[None, :] >= start_rows) & (grid_rows[None, :] < start_rows + P_SIZE)).astype(jnp.float32)
    cover_cols = ((grid_cols[None, :] >= start_cols) & (grid_cols[None, :] < start_cols + P_SIZE)).astype(jnp.float32)
    coverage = jnp.dot(cover_rows.T, cover_cols, precision=lax.Precision.HIGHEST)
    averaged = summed / jnp.maximum(coverage, 1.0)[None, :, :]
    return (mean_field.astype(jnp.float32) + averaged).astype(jnp.bfloat16)
```

```python
import jax
import jax.numpy as jnp
from jax import lax
from jax.sharding import PartitionSpec as P

P_SIZE = 32
PPD = 1


def from_behind(block, axis, distance):
    devices = range(lax.axis_size(axis))
    route = [(i - distance, i) for i in devices if i - distance in devices]
    return lax.ppermute(block, axis, route)


def from_diagonal(block):
    bands = lax.axis_size("band")
    sects = lax.axis_size("sect")
    route = [
        (b * sects + s, (b + 1) * sects + s + 1) for b in range(bands - 1) for s in range(sects - 1)
    ]
    return lax.ppermute(block, ("band", "sect"), route)


def conv(values, weight, padding):
    kernel = weight.reshape(3, 3, weight.shape[1], weight.shape[2])
    return lax.conv_general_dilated(
        values,
        kernel,
        (1, 1),
        padding,
        dimension_numbers=("NHWC", "HWOI", "NHWC"),
        preferred_element_type=jnp.float32,
    )


def slots_of(anchors, band, sect, row_count, band_total, sect_total, per_reader, capacity):
    view = anchors.reshape(band_total, sect_total * per_reader, 2)
    column = lax.dynamic_slice_in_dim(view, sect * per_reader, per_reader, 1)
    column = column.reshape(band_total * per_reader, 2)
    owned = column[:, 0] // row_count == band
    listing = jnp.arange(band_total * per_reader, dtype=jnp.int32)
    earlier = owned[None, :] & (listing[None, :] < listing[:, None])
    order = jnp.sum(earlier.astype(jnp.int32), axis=1)
    chosen = owned[None, :] & (order[None, :] == jnp.arange(capacity, dtype=jnp.int32)[:, None])
    present = jnp.any(chosen, axis=1)
    rows = jnp.sum(jnp.where(chosen, column[None, :, 0], 0), axis=1)
    cols = jnp.sum(jnp.where(chosen, column[None, :, 1], 0), axis=1)
    index = jnp.sum(jnp.where(chosen, listing[None, :], 0), axis=1)
    return present, rows, cols, index


def inside_mask(row_first, col_first, rows, cols, row_limit, col_limit):
    r = row_first + jnp.arange(rows, dtype=jnp.int32)
    c = col_first + jnp.arange(cols, dtype=jnp.int32)
    return ((r >= 0) & (r < row_limit))[:, None] & ((c >= 0) & (c < col_limit))[None, :]


def regression(wide, keep, w_in, b_in, w_out, b_out):
    hidden = jax.nn.silu(conv(wide, w_in, "VALID") + b_in)
    hidden = jnp.where(keep[..., None], hidden, 0.0).astype(jnp.bfloat16)
    middle = wide[:, 2:-2, 2:-2].astype(jnp.float32)
    return (middle + conv(hidden, w_out, "VALID") + b_out).astype(jnp.bfloat16)


def denoise(mean, noises, weight_in, biases, weight_out, out_bias):
    start_mean = mean.astype(jnp.float32)
    state = start_mean + noises[:, 0].astype(jnp.float32)
    steps_total = noises.shape[1]
    for step in range(steps_total):
        inner = state.astype(jnp.bfloat16)
        hidden = jax.nn.silu(conv(inner, weight_in, "SAME") + biases[step]).astype(jnp.bfloat16)
        state = state - 0.5 * (conv(hidden, weight_out, "SAME") + out_bias)
        if step + 1 < steps_total:
            state = state + 0.5 * noises[:, step + 1].astype(jnp.float32)
    return (state - start_mean).astype(jnp.bfloat16)


def per_device(
    state_field,
    conv_in_weight,
    conv_in_bias,
    conv_out_weight,
    conv_out_bias,
    patch_anchor,
    patch_noise,
    denoise_in_weight,
    step_bias,
    denoise_out_weight,
    denoise_bias,
):
    band_total = lax.axis_size("band")
    sect_total = lax.axis_size("sect")
    band_index = lax.axis_index("band")
    sect_index = lax.axis_index("sect")
    channels, row_count, col_count = state_field.shape
    row_limit = row_count * band_total
    col_limit = col_count * sect_total
    side = P_SIZE
    per_reader = PPD
    capacity = 2 * PPD
    steps_total = patch_noise.shape[1]

    noise_list = lax.all_gather(patch_noise, "band", axis=0, tiled=True)

    state = jnp.transpose(state_field, (1, 2, 0))
    parts = [from_behind(state[-2:], "band", 1), state]
    need, distance = side + 1, 1
    while need > 0:
        take = min(need, row_count)
        parts.append(from_behind(state[:take], "band", -distance))
        need, distance = need - take, distance + 1
    tall = jnp.concatenate(parts, axis=0)
    left = from_behind(tall[:, -2:], "sect", 1)
    right = from_behind(tall[:, : side + 1], "sect", -1)
    full = jnp.concatenate([left, tall, right], axis=1)

    def slots_at(band, sect):
        return slots_of(
            patch_anchor, band, sect, row_count, band_total, sect_total, per_reader, capacity
        )

    first_row = band_index * row_count
    first_col = sect_index * col_count
    present, rows, cols, index = slots_at(band_index, sect_index)
    windows = []
    keeps = []
    noises = []
    for slot in range(capacity):
        windows.append(
            lax.dynamic_slice(
                full,
                (rows[slot] - first_row, cols[slot] - first_col, 0),
                (side + 4, side + 4, channels),
            )
        )
        keeps.append(
            inside_mask(
                rows[slot] - 1, cols[slot] - 1, side + 2, side + 2, row_limit, col_limit
            )
        )
        noises.append(lax.dynamic_index_in_dim(noise_list, index[slot], 0, keepdims=False))
    noise = jnp.stack(noises).reshape(capacity, steps_total, channels, side, side)
    noise = jnp.transpose(noise, (0, 1, 3, 4, 2))
    regression_weights = (conv_in_weight, conv_in_bias, conv_out_weight, conv_out_bias)
    patch_mean = regression(jnp.stack(windows), jnp.stack(keeps), *regression_weights)
    correction = denoise(
        patch_mean, noise, denoise_in_weight, step_bias, denoise_out_weight, denoise_bias
    )
    correction = jnp.where(present[:, None, None, None], correction, jnp.zeros_like(correction))

    pieces = [
        (correction, slots_at(band_index, sect_index)),
        (from_behind(correction, "sect", 1), slots_at(band_index, sect_index - 1)),
        (from_behind(correction, "band", 1), slots_at(band_index - 1, sect_index)),
        (from_diagonal(correction), slots_at(band_index - 1, sect_index - 1)),
    ]

    keep = inside_mask(
        first_row - 1, first_col - 1, row_count + 2, col_count + 2, row_limit, col_limit
    )
    wide = full[None, : row_count + 4, : col_count + 4]
    mean_field = regression(wide, keep[None], *regression_weights)[0]

    placed = []
    selects = []
    offsets = jnp.arange(side, dtype=jnp.int32)
    columns = jnp.arange(col_count, dtype=jnp.int32)
    for values, (_, piece_rows, piece_cols, _) in pieces:
        padded = jnp.pad(values, ((0, 0), (row_count, row_count), (0, 0), (0, 0)))
        for slot in range(capacity):
            start = row_count - (piece_rows[slot] - first_row)
            placed.append(lax.dynamic_slice_in_dim(padded[slot], start, row_count, 0))
            at = piece_cols[slot] - first_col + offsets
            selects.append((at[:, None] == columns[None, :]).astype(jnp.bfloat16))
    stacked = jnp.concatenate(placed, axis=1)
    select = jnp.concatenate(selects, axis=0)
    summed = jnp.einsum("rqc,qk->crk", stacked, select, preferred_element_type=jnp.float32)

    grid_rows = first_row + jnp.arange(row_count, dtype=jnp.int32)
    grid_cols = first_col + jnp.arange(col_count, dtype=jnp.int32)
    start_rows = patch_anchor[:, 0:1]
    start_cols = patch_anchor[:, 1:2]
    cover_rows = (
        (grid_rows[None, :] >= start_rows) & (grid_rows[None, :] < start_rows + side)
    ).astype(jnp.float32)
    cover_cols = (
        (grid_cols[None, :] >= start_cols) & (grid_cols[None, :] < start_cols + side)
    ).astype(jnp.float32)
    coverage = jnp.dot(cover_rows.T, cover_cols, precision=lax.Precision.HIGHEST)
    averaged = summed / jnp.maximum(coverage, 1.0)[None, :, :]
    mean_first = jnp.transpose(mean_field, (2, 0, 1)).astype(jnp.float32)
    return (mean_first + averaged).astype(jnp.bfloat16)


def solution(mesh):
    placed = (
        P("groups", "band", "sect"),
        P(),
        P(),
        P(),
        P(),
        P("groups", None),
        P(("groups", "band", "sect"), None, None, None),
        P(),
        P(),
        P(),
        P(),
    )
    return jax.shard_map(
        per_device,
        mesh=mesh,
        in_specs=placed,
        out_specs=P("groups", "band", "sect"),
        check_vma=False,
    )
```

```python
import functools

import jax
import jax.numpy as jnp
from jax import lax
from jax.experimental import pallas as pl
from jax.experimental.pallas import tpu as pltpu
from jax.sharding import PartitionSpec as P

P_SIZE = 32
PPD = 1


def from_behind(block, axis, distance):
    devices = range(lax.axis_size(axis))
    route = [(i - distance, i) for i in devices if i - distance in devices]
    return lax.ppermute(block, axis, route)


def from_diagonal(block):
    bands = lax.axis_size("band")
    sects = lax.axis_size("sect")
    route = [
        (b * sects + s, (b + 1) * sects + s + 1) for b in range(bands - 1) for s in range(sects - 1)
    ]
    return lax.ppermute(block, ("band", "sect"), route)


def conv(values, weight, padding):
    kernel = weight.reshape(3, 3, weight.shape[1], weight.shape[2])
    return lax.conv_general_dilated(
        values,
        kernel,
        (1, 1),
        padding,
        dimension_numbers=("NHWC", "HWOI", "NHWC"),
        preferred_element_type=jnp.float32,
    )


def slot_table(anchors, bands, sects, row_count, sect_total, per_reader, capacity):
    listing = jnp.arange(anchors.shape[0], dtype=jnp.int32)
    sector = (listing // per_reader) % sect_total
    owner = anchors[:, 0] // row_count
    owned = (owner[None, :] == bands[:, None]) & (sector[None, :] == sects[:, None])
    earlier = owned[:, None, :] & (listing[None, None, :] < listing[None, :, None])
    order = jnp.sum(earlier.astype(jnp.int32), axis=2)
    slot = jnp.arange(capacity, dtype=jnp.int32)
    chosen = owned[:, None, :] & (order[:, None, :] == slot[None, :, None])
    place = (listing // (per_reader * sect_total)) * per_reader + listing % per_reader
    columns = jnp.stack(
        [anchors[:, 0], anchors[:, 1], place, jnp.ones_like(place)], axis=1
    )
    table = jnp.sum(jnp.where(chosen[..., None], columns[None, None], 0), axis=2)
    return table.reshape(bands.shape[0] * capacity, 4)


def place_kernel(
    channels, margin, table_ref, own_ref, left_ref, above_ref, diagonal_ref, mean_ref, out_ref
):
    capacity, side = own_ref.shape[0], own_ref.shape[1]
    row_count, col_count, _ = out_ref.shape
    sources = (own_ref, left_ref, above_ref, diagonal_ref)
    depth = len(sources) * capacity * side
    lane = lax.broadcasted_iota(jnp.int32, (col_count, depth), 1)
    cell = lax.broadcasted_iota(jnp.int32, (col_count, depth), 0)
    at = jnp.zeros_like(lane)
    for slot in range(len(sources) * capacity):
        within = (lane >= slot * side) & (lane < (slot + 1) * side)
        at = jnp.where(within, lane - slot * side + table_ref[slot, 1], at)
    select = jnp.where(at == cell, 1.0, 0.0).astype(jnp.bfloat16)

    def one_row(r, carry):
        values = []
        for number, source in enumerate(sources):
            for slot in range(capacity):
                row = r - table_ref[number * capacity + slot, 0]
                inside = (row >= 0) & (row < side)
                taken = source[slot, jnp.clip(row, 0, side - 1)]
                values.append(jnp.where(inside, taken, jnp.zeros_like(taken)))
        summed = jnp.dot(
            select, jnp.concatenate(values, axis=0), preferred_element_type=jnp.float32
        )
        coverage = jnp.maximum(summed[:, channels : channels + 1], 1.0)
        mean = mean_ref[r, margin : margin + col_count].astype(jnp.float32)
        out_ref[r] = (mean + summed / coverage).astype(out_ref.dtype)
        return carry

    lax.fori_loop(0, row_count, one_row, 0, unroll=2)


def inside_mask(row_first, col_first, rows, cols, row_limit, col_limit):
    r = row_first + jnp.arange(rows, dtype=jnp.int32)
    c = col_first + jnp.arange(cols, dtype=jnp.int32)
    return ((r >= 0) & (r < row_limit))[:, None] & ((c >= 0) & (c < col_limit))[None, :]


def regression(wide, keep, w_in, b_in, w_out, b_out, padding, col_cut):
    hidden = jax.nn.silu(conv(wide, w_in, padding) + b_in)
    hidden = jnp.where(keep[..., None], hidden, 0.0).astype(jnp.bfloat16)
    middle = wide[:, 2:-2, col_cut : wide.shape[2] - col_cut].astype(jnp.float32)
    return (middle + conv(hidden, w_out, padding) + b_out).astype(jnp.bfloat16)


def denoise(mean, noises, weight_in, biases, weight_out, out_bias):
    start_mean = mean.astype(jnp.float32)
    state = start_mean + noises[:, 0].astype(jnp.float32)
    steps_total = noises.shape[1]
    for step in range(steps_total):
        inner = state.astype(jnp.bfloat16)
        hidden = jax.nn.silu(conv(inner, weight_in, "SAME") + biases[step]).astype(jnp.bfloat16)
        state = state - 0.5 * (conv(hidden, weight_out, "SAME") + out_bias)
        if step + 1 < steps_total:
            state = state + 0.5 * noises[:, step + 1].astype(jnp.float32)
    return (state - start_mean).astype(jnp.bfloat16)


def per_device(
    state_field,
    conv_in_weight,
    conv_in_bias,
    conv_out_weight,
    conv_out_bias,
    patch_anchor,
    patch_noise,
    denoise_in_weight,
    step_bias,
    denoise_out_weight,
    denoise_bias,
):
    band_total = lax.axis_size("band")
    sect_total = lax.axis_size("sect")
    band_index = lax.axis_index("band")
    sect_index = lax.axis_index("sect")
    channels, row_count, col_count = state_field.shape
    row_limit = row_count * band_total
    col_limit = col_count * sect_total
    side = P_SIZE
    per_reader = PPD
    capacity = 2 * PPD
    steps_total = patch_noise.shape[1]
    lanes = (channels // 128 + 1) * 128
    extra = lanes - channels
    margin = 16
    beyond = (side // 16 + 1) * 16

    noise_list = lax.all_gather(patch_noise, "band", axis=0, tiled=True)

    state = jnp.pad(jnp.transpose(state_field, (1, 2, 0)), ((0, 0), (0, 0), (0, extra)))
    parts = [from_behind(state[-2:], "band", 1), state]
    need, distance = side + 1, 1
    while need > 0:
        take = min(need, row_count)
        parts.append(from_behind(state[:take], "band", -distance))
        need, distance = need - take, distance + 1
    tall = jnp.concatenate(parts, axis=0)
    left = from_behind(tall[:, -margin:], "sect", 1)
    right = from_behind(tall[:, :beyond], "sect", -1)
    full = jnp.concatenate([left, tall, right], axis=1)

    first_row = band_index * row_count
    first_col = sect_index * col_count
    back = jnp.arange(4, dtype=jnp.int32)
    table = slot_table(
        patch_anchor,
        band_index - back // 2,
        sect_index - back % 2,
        row_count,
        sect_total,
        per_reader,
        capacity,
    )
    w_in = jnp.pad(conv_in_weight, ((0, 0), (0, 0), (0, extra)))
    w_out = jnp.pad(conv_out_weight, ((0, 0), (0, extra), (0, 0)))
    b_out = jnp.pad(conv_out_bias, (0, extra))
    d_in = jnp.pad(denoise_in_weight, ((0, 0), (0, 0), (0, extra)))
    d_out = jnp.pad(denoise_out_weight, ((0, 0), (0, extra), (0, 0)))
    d_bias = jnp.pad(denoise_bias, (0, extra))

    windows = []
    keeps = []
    noises = []
    for slot in range(capacity):
        row, col = table[slot, 0], table[slot, 1]
        windows.append(
            lax.dynamic_slice(
                full,
                (row - first_row, col - first_col + margin - 2, 0),
                (side + 4, side + 4, lanes),
            )
        )
        keeps.append(inside_mask(row - 1, col - 1, side + 2, side + 2, row_limit, col_limit))
        noises.append(lax.dynamic_index_in_dim(noise_list, table[slot, 2], 0, keepdims=False))
    noise = jnp.transpose(jnp.stack(noises), (0, 1, 3, 2))
    noise = jnp.pad(noise, ((0, 0), (0, 0), (0, 0), (0, extra)))
    noise = noise.reshape(capacity, steps_total, side, side, lanes)
    window = jnp.stack(windows)
    patch_mean = regression(
        window, jnp.stack(keeps), w_in, conv_in_bias, w_out, b_out, "VALID", 2
    )
    correction = denoise(patch_mean, noise, d_in, step_bias, d_out, d_bias)
    present = table[:capacity, 3][:, None, None, None] > 0
    spare = jnp.arange(lanes, dtype=jnp.int32) == channels
    correction = jnp.where(spare, jnp.ones_like(correction), correction)
    correction = jnp.where(present, correction, jnp.zeros_like(correction))

    pieces = [
        correction,
        from_behind(correction, "sect", 1),
        from_behind(correction, "band", 1),
        from_diagonal(correction),
    ]

    width = full.shape[1]
    keep = inside_mask(
        first_row - 1, first_col - margin, row_count + 2, width, row_limit, col_limit
    )
    mean_field = regression(
        full[None, : row_count + 4],
        keep[None],
        w_in,
        conv_in_bias,
        w_out,
        b_out,
        ((0, 0), (1, 1)),
        0,
    )[0]

    origin = jnp.stack([first_row, first_col]).astype(jnp.int32)
    relative = table[:, :2] - origin[None, :]
    vmem = pl.BlockSpec(memory_space=pltpu.VMEM)
    result = pl.pallas_call(
        functools.partial(place_kernel, channels, margin),
        out_shape=jax.ShapeDtypeStruct((row_count, col_count, lanes), jnp.bfloat16),
        in_specs=[pl.BlockSpec(memory_space=pltpu.SMEM)] + [vmem] * 5,
        out_specs=vmem,
        compiler_params=pltpu.CompilerParams(vmem_limit_bytes=24 * 1024 * 1024),
    )(relative, *pieces, mean_field)
    return jnp.transpose(result[:, :, :channels], (2, 0, 1))


def solution(mesh):
    placed = (
        P("groups", "band", "sect"),
        P(),
        P(),
        P(),
        P(),
        P("groups", None),
        P(("groups", "band", "sect"), None, None, None),
        P(),
        P(),
        P(),
        P(),
    )
    return jax.shard_map(
        per_device,
        mesh=mesh,
        in_specs=placed,
        out_specs=P("groups", "band", "sect"),
        check_vma=False,
    )
```

```python
import functools

import jax
import jax.numpy as jnp
from jax import lax
from jax.experimental import pallas as pl
from jax.experimental.pallas import tpu as pltpu
from jax.sharding import PartitionSpec as P

P_SIZE = 32
PPD = 1


def from_behind(block, axis, distance):
    devices = range(lax.axis_size(axis))
    route = [(i - distance, i) for i in devices if i - distance in devices]
    return lax.ppermute(block, axis, route)


def from_diagonal(block):
    bands = lax.axis_size("band")
    sects = lax.axis_size("sect")
    route = [
        (b * sects + s, (b + 1) * sects + s + 1) for b in range(bands - 1) for s in range(sects - 1)
    ]
    return lax.ppermute(block, ("band", "sect"), route)


def conv(values, weight, padding):
    kernel = weight.reshape(3, 3, weight.shape[1], weight.shape[2])
    return lax.conv_general_dilated(
        values,
        kernel,
        (1, 1),
        padding,
        dimension_numbers=("NHWC", "HWOI", "NHWC"),
        preferred_element_type=jnp.float32,
    )


def slot_table(anchors, bands, sects, row_count, sect_total, per_reader, capacity):
    listing = jnp.arange(anchors.shape[0], dtype=jnp.int32)
    sector = (listing // per_reader) % sect_total
    owner = anchors[:, 0] // row_count
    owned = (owner[None, :] == bands[:, None]) & (sector[None, :] == sects[:, None])
    earlier = owned[:, None, :] & (listing[None, None, :] < listing[None, :, None])
    order = jnp.sum(earlier.astype(jnp.int32), axis=2)
    slot = jnp.arange(capacity, dtype=jnp.int32)
    chosen = owned[:, None, :] & (order[:, None, :] == slot[None, :, None])
    place = (listing // (per_reader * sect_total)) * per_reader + listing % per_reader
    columns = jnp.stack(
        [anchors[:, 0], anchors[:, 1], place, jnp.ones_like(place)], axis=1
    )
    table = jnp.sum(jnp.where(chosen[..., None], columns[None, None], 0), axis=2)
    return table.reshape(bands.shape[0] * capacity, 4)


def place_kernel(
    channels, margin, table_ref, own_ref, left_ref, above_ref, diagonal_ref, mean_ref, out_ref
):
    capacity, side = own_ref.shape[0], own_ref.shape[1]
    row_count, col_count, _ = out_ref.shape
    sources = (own_ref, left_ref, above_ref, diagonal_ref)
    depth = len(sources) * capacity * side
    lane = lax.broadcasted_iota(jnp.int32, (col_count, depth), 1)
    cell = lax.broadcasted_iota(jnp.int32, (col_count, depth), 0)
    at = jnp.zeros_like(lane)
    for slot in range(len(sources) * capacity):
        within = (lane >= slot * side) & (lane < (slot + 1) * side)
        at = jnp.where(within, lane - slot * side + table_ref[slot, 1], at)
    select = jnp.where(at == cell, 1.0, 0.0).astype(jnp.bfloat16)

    def one_row(r, carry):
        values = []
        for number, source in enumerate(sources):
            for slot in range(capacity):
                row = r - table_ref[number * capacity + slot, 0]
                inside = (row >= 0) & (row < side)
                taken = source[slot, jnp.clip(row, 0, side - 1)]
                values.append(jnp.where(inside, taken, jnp.zeros_like(taken)))
        summed = jnp.dot(
            select, jnp.concatenate(values, axis=0), preferred_element_type=jnp.float32
        )
        coverage = jnp.maximum(summed[:, channels : channels + 1], 1.0)
        mean = mean_ref[r, margin : margin + col_count].astype(jnp.float32)
        out_ref[r] = (mean + summed / coverage).astype(out_ref.dtype)
        return carry

    lax.fori_loop(0, row_count, one_row, 0, unroll=2)


def inside_mask(row_first, col_first, rows, cols, row_limit, col_limit):
    r = row_first + jnp.arange(rows, dtype=jnp.int32)
    c = col_first + jnp.arange(cols, dtype=jnp.int32)
    return ((r >= 0) & (r < row_limit))[:, None] & ((c >= 0) & (c < col_limit))[None, :]


def regression(wide, keep, w_in, b_in, w_out, b_out, padding, col_cut):
    hidden = jax.nn.silu(conv(wide, w_in, padding) + b_in)
    hidden = jnp.where(keep[..., None], hidden, 0.0).astype(jnp.bfloat16)
    middle = wide[:, 2:-2, col_cut : wide.shape[2] - col_cut].astype(jnp.float32)
    return (middle + conv(hidden, w_out, padding) + b_out).astype(jnp.bfloat16)


def tap_matrix(weight):
    taps, outputs, inputs = weight.shape
    grid = weight.reshape(3, 3, outputs, inputs)
    return jnp.transpose(grid, (0, 3, 1, 2)).reshape(3 * inputs, 3 * outputs)


def conv_row(ref, r, weight_ref):
    rows = jnp.concatenate([ref[r], ref[r + 1], ref[r + 2]], axis=1)
    terms = jnp.dot(rows, weight_ref[...], preferred_element_type=jnp.float32)
    width = terms.shape[0]
    outputs = terms.shape[1] // 3
    before = pltpu.roll(terms[:, :outputs], 1, 0)
    after = pltpu.roll(terms[:, 2 * outputs :], width - 1, 0)
    return before + terms[:, outputs : 2 * outputs] + after


def regression_kernel(
    row_limit, col_limit, margin, origin_ref, full_ref, w_in, b_in, w_out, b_out, out_ref, hidden_ref
):
    width = full_ref.shape[1]
    first_row = origin_ref[0] - 1
    cols = lax.broadcasted_iota(jnp.int32, (width, hidden_ref.shape[2]), 0)
    cols = cols + (origin_ref[1] - margin)

    def hidden_row(r, carry):
        act = jax.nn.silu(conv_row(full_ref, r, w_in) + b_in[...])
        row = jnp.full_like(cols, first_row + r)
        keep = (cols >= 0) & (cols < col_limit) & (row >= 0) & (row < row_limit)
        hidden_ref[r] = jnp.where(keep, act, 0.0).astype(hidden_ref.dtype)
        return carry

    def mean_row(r, carry):
        value = full_ref[r + 2].astype(jnp.float32) + conv_row(hidden_ref, r, w_out)
        out_ref[r] = (value + b_out[...]).astype(out_ref.dtype)
        return carry

    lax.fori_loop(0, hidden_ref.shape[0], hidden_row, 0, unroll=2)
    lax.fori_loop(0, out_ref.shape[0], mean_row, 0, unroll=2)


def denoise(mean, noises, weight_in, biases, weight_out, out_bias):
    start_mean = mean.astype(jnp.float32)
    state = start_mean + noises[:, 0].astype(jnp.float32)
    steps_total = noises.shape[1]
    for step in range(steps_total):
        inner = state.astype(jnp.bfloat16)
        hidden = jax.nn.silu(conv(inner, weight_in, "SAME") + biases[step]).astype(jnp.bfloat16)
        state = state - 0.5 * (conv(hidden, weight_out, "SAME") + out_bias)
        if step + 1 < steps_total:
            state = state + 0.5 * noises[:, step + 1].astype(jnp.float32)
    return (state - start_mean).astype(jnp.bfloat16)


def per_device(
    state_field,
    conv_in_weight,
    conv_in_bias,
    conv_out_weight,
    conv_out_bias,
    patch_anchor,
    patch_noise,
    denoise_in_weight,
    step_bias,
    denoise_out_weight,
    denoise_bias,
):
    band_total = lax.axis_size("band")
    sect_total = lax.axis_size("sect")
    band_index = lax.axis_index("band")
    sect_index = lax.axis_index("sect")
    channels, row_count, col_count = state_field.shape
    row_limit = row_count * band_total
    col_limit = col_count * sect_total
    side = P_SIZE
    per_reader = PPD
    capacity = 2 * PPD
    steps_total = patch_noise.shape[1]
    lanes = (channels // 128 + 1) * 128
    extra = lanes - channels
    margin = 16
    beyond = (side // 16 + 1) * 16

    noise_list = lax.all_gather(patch_noise, "band", axis=0, tiled=True)

    state = jnp.pad(jnp.transpose(state_field, (1, 2, 0)), ((0, 0), (0, 0), (0, extra)))
    parts = [from_behind(state[-2:], "band", 1), state]
    need, distance = side + 1, 1
    while need > 0:
        take = min(need, row_count)
        parts.append(from_behind(state[:take], "band", -distance))
        need, distance = need - take, distance + 1
    tall = jnp.concatenate(parts, axis=0)
    left = from_behind(tall[:, -margin:], "sect", 1)
    right = from_behind(tall[:, :beyond], "sect", -1)
    full = jnp.concatenate([left, tall, right], axis=1)

    first_row = band_index * row_count
    first_col = sect_index * col_count
    back = jnp.arange(4, dtype=jnp.int32)
    table = slot_table(
        patch_anchor,
        band_index - back // 2,
        sect_index - back % 2,
        row_count,
        sect_total,
        per_reader,
        capacity,
    )
    w_in = jnp.pad(conv_in_weight, ((0, 0), (0, 0), (0, extra)))
    w_out = jnp.pad(conv_out_weight, ((0, 0), (0, extra), (0, 0)))
    b_out = jnp.pad(conv_out_bias, (0, extra))
    d_in = jnp.pad(denoise_in_weight, ((0, 0), (0, 0), (0, extra)))
    d_out = jnp.pad(denoise_out_weight, ((0, 0), (0, extra), (0, 0)))
    d_bias = jnp.pad(denoise_bias, (0, extra))

    windows = []
    keeps = []
    noises = []
    for slot in range(capacity):
        row, col = table[slot, 0], table[slot, 1]
        windows.append(
            lax.dynamic_slice(
                full,
                (row - first_row, col - first_col + margin - 2, 0),
                (side + 4, side + 4, lanes),
            )
        )
        keeps.append(inside_mask(row - 1, col - 1, side + 2, side + 2, row_limit, col_limit))
        noises.append(lax.dynamic_index_in_dim(noise_list, table[slot, 2], 0, keepdims=False))
    noise = jnp.transpose(jnp.stack(noises), (0, 1, 3, 2))
    noise = jnp.pad(noise, ((0, 0), (0, 0), (0, 0), (0, extra)))
    noise = noise.reshape(capacity, steps_total, side, side, lanes)
    window = jnp.stack(windows)
    patch_mean = regression(
        window, jnp.stack(keeps), w_in, conv_in_bias, w_out, b_out, "VALID", 2
    )
    correction = denoise(patch_mean, noise, d_in, step_bias, d_out, d_bias)
    present = table[:capacity, 3][:, None, None, None] > 0
    spare = jnp.arange(lanes, dtype=jnp.int32) == channels
    correction = jnp.where(spare, jnp.ones_like(correction), correction)
    correction = jnp.where(present, correction, jnp.zeros_like(correction))

    pieces = [
        correction,
        from_behind(correction, "sect", 1),
        from_behind(correction, "band", 1),
        from_diagonal(correction),
    ]

    origin = jnp.stack([first_row, first_col]).astype(jnp.int32)
    relative = table[:, :2] - origin[None, :]
    vmem = pl.BlockSpec(memory_space=pltpu.VMEM)
    smem = pl.BlockSpec(memory_space=pltpu.SMEM)
    width = full.shape[1]
    hidden_lanes = conv_in_weight.shape[1]
    mean_field = pl.pallas_call(
        functools.partial(regression_kernel, row_limit, col_limit, margin),
        out_shape=jax.ShapeDtypeStruct((row_count, width, lanes), jnp.bfloat16),
        in_specs=[smem] + [vmem] * 5,
        out_specs=vmem,
        scratch_shapes=[pltpu.VMEM((row_count + 2, width, hidden_lanes), jnp.bfloat16)],
        cost_estimate=pl.CostEstimate(
            flops=36 * row_count * width * lanes * hidden_lanes,
            bytes_accessed=4 * full.size,
            transcendentals=row_count * width * hidden_lanes,
        ),
        compiler_params=pltpu.CompilerParams(vmem_limit_bytes=24 * 1024 * 1024),
    )(origin, full, tap_matrix(w_in), conv_in_bias[None], tap_matrix(w_out), b_out[None])
    result = pl.pallas_call(
        functools.partial(place_kernel, channels, margin),
        out_shape=jax.ShapeDtypeStruct((row_count, col_count, lanes), jnp.bfloat16),
        in_specs=[smem] + [vmem] * 5,
        out_specs=vmem,
        compiler_params=pltpu.CompilerParams(vmem_limit_bytes=24 * 1024 * 1024),
    )(relative, *pieces, mean_field)
    return jnp.transpose(result[:, :, :channels], (2, 0, 1))


def solution(mesh):
    placed = (
        P("groups", "band", "sect"),
        P(),
        P(),
        P(),
        P(),
        P("groups", None),
        P(("groups", "band", "sect"), None, None, None),
        P(),
        P(),
        P(),
        P(),
    )
    return jax.shard_map(
        per_device,
        mesh=mesh,
        in_specs=placed,
        out_specs=P("groups", "band", "sect"),
        check_vma=False,
    )
```
